128 devices in a mesh: ty: 8 (over x, core), tx: 16 (over y, z).
Axes of the slice: x: 4, y: 4, z: 4, core: 2. Of those that a mesh axis runs over, the one named last changes fastest.
Arguments:
- amplitudes: bfloat16 [4096, 256, 256], P(('ty', 'tx')), may hold values from 0.099609375 to 4
- owners: int32 [4096, 1], P(('ty', 'tx')), may hold values from 0 to 15; in each aligned block of 32 rows (0 to 31, 32 to 63, ...) at most 3 rows name the same one
- offsets: int32 [4096, 2], P(('ty', 'tx')), may hold values from 0 to 511
- object_field: float32 [2, 4096, 8192], P(None, 'ty', 'tx'), may hold values from -6 to 6
- probe: float32 [2, 256, 256], replicated, may hold values from -6 to 6
Outputs:
- object_new: float32 [2, 4096, 8192], P(None, 'ty', 'tx')
- probe_step: float32 [2, 256, 256], replicated
The draws below stay inside these ranges and needn't reach their ends.
Inputs may be any that keep to these rules, and one draw needn't show every extreme that they name: `owners`: among the patterns of one device no owner column is named more than 3 times, a bound that some block reaches.
All inputs are finite; a program needn't handle non-finite values.
Results may differ from the reference program's by a relative error of at most 0.0013.
The reference program's roundings to bfloat16 on the way count: a program that leaves them out, or rounds other values in their place, can miss the bound.
Values may be sent and summed in bfloat16 or wider, within the bound.
A program may use at most 320 MiB of HBM per device.

```python
import math
import jax
import jax.numpy as jnp
import numpy as np
from jax import lax

P_SIZE = 256
TILE = 512
PAT_DEV = 32
CAP = 3
PATTERNS = 4096
NY = 4096
NX = 8192
N_TX = 16


def touch_ends(values, stream_key, low, high):
    dims = values.shape
    index_at = [jax.random.randint(jax.random.fold_in(stream_key, axis), (), 0, dims[axis]) for axis in range(len(dims))]
    values = values.at[tuple(index_at)].set(low)
    longest = dims.index(max(dims))
    index_at[longest] = (index_at[longest] + 1) % dims[longest]
    return values.at[tuple(index_at)].set(high)


def levels(own_key, shape, pieces, least, high):
    loudness = 1.0
    for axis_at, parts in pieces:
        heights = jax.random.uniform(jax.random.fold_in(jax.random.fold_in(own_key, 6), axis_at), (parts,), jnp.float32, least / len(pieces), high / len(pieces))
        loudness = loudness * jnp.repeat(jnp.exp(heights), shape[axis_at] // parts).reshape((-1,) + (1,) * (len(shape) - 1 - axis_at))
    return loudness


def deal_out(key, own, number, rows, amount, top, most, lean):
    ranking = jax.random.permutation(key, amount)
    crowded, usual = shares(amount, rows * top, most, lean, True), shares(amount, rows * top, most, lean, False)
    places = jnp.arange(amount)

    def named(tallies, turn):
        used = int((tallies > 0).sum())
        fixed = max(1, used // 4)
        moved = fixed + (places - fixed + turn * (used - fixed)) % max(1, amount - fixed)
        return jnp.zeros((amount,), jnp.int32).at[ranking[jnp.where(places < fixed, places, moved)]].set(jnp.asarray(tallies, jnp.int32))

    tallies = jnp.where(number % 4 == 0, named(crowded, number // 4), named(usual, number - number // 4 - 1))
    mixed = jax.random.permutation(jax.random.fold_in(own, 3), amount)
    source_of, receiver = mixed[0:amount // 2 * 2:2], mixed[1:amount // 2 * 2:2]
    room = jnp.minimum(tallies[source_of] - 1, most - tallies[receiver]) // 2
    room = jnp.where((source_of == ranking[0]) | (receiver == ranking[0]) | (tallies[receiver] == 0), 0, jnp.maximum(room, 0))
    moved = jax.random.randint(jax.random.fold_in(own, 4), (amount // 2,), 0, 1 << 20) % (room + 1)
    tallies = tallies.at[source_of].add(-moved).at[receiver].add(moved)
    items = jnp.searchsorted(jnp.cumsum(tallies), jnp.arange(rows * top), side="right").astype(jnp.int32)
    listing = items.reshape(top, rows).T
    listing = listing[jax.random.permutation(jax.random.fold_in(own, 1), rows)]
    turn = jax.random.randint(jax.random.fold_in(own, 2), (rows, 1), 0, top)
    return jnp.take_along_axis(listing, (jnp.arange(top)[None, :] + turn) % top, axis=1)


def shares(count, total, limit, slope, full):
    weights = [(1 << 20) // math.isqrt(grade ** slope) + 1 for grade in range(1, count + 1)]
    largest = limit if full else min(limit, max(-(-total // count), total * weights[0] // sum(weights)))
    least = 1 if total - largest >= count - 1 else 0
    given, surplus = [largest] + [least] * (count - 1), total - largest - least * (count - 1)
    while surplus > 0:
        free = [i for i in range(1, count) if given[i] < largest] or [i for i in range(1, count) if given[i] < limit]
        pool, remaining = sum([weights[i] for i in free]), surplus
        for i in free:
            more = min(limit - given[i], max(1, remaining * weights[i] // pool), surplus)
            given[i] = given[i] + more
            surplus = surplus - more
    return np.array(given)


def gaussian(stream_key, shape, scale, limit, shards=(), held_as=jnp.bfloat16):
    entries = jax.random.normal(stream_key, shape, jnp.float32) * scale
    if len(shards) > 0:
        entries = levels(stream_key, shape, shards, -0.22, 0.18) * entries
    return jnp.clip(entries, min=-limit, max=limit).astype(held_as)


def setup_inputs(seed: int = 0) -> dict:
    splits = jax.random.split(jax.random.key(seed), 6)
    amplitudes = jnp.clip(jnp.exp(math.log(4.0) - 3.6927934 * jax.random.uniform(splits[0], (PATTERNS, P_SIZE, P_SIZE), jnp.float32) ** levels(splits[0], (PATTERNS, P_SIZE, P_SIZE), ((0, 128),), -0.2, 0.2)), 0.099609375, 4.0).astype(jnp.bfloat16)
    owners_keys = jax.random.split(jax.random.fold_in(splits[1], 1), PATTERNS // PAT_DEV)
    owners_turns = jax.random.permutation(jax.random.fold_in(splits[1], 3), PATTERNS // PAT_DEV)
    owners = jax.vmap(lambda own, number: deal_out(jax.random.fold_in(splits[1], 2), own, number, PAT_DEV, N_TX, 1, CAP, 2))(owners_keys, owners_turns).reshape((PATTERNS, 1))
    offsets = touch_ends(jax.random.randint(splits[2], (PATTERNS, 2), 0, TILE), jax.random.fold_in(splits[2], 1), 0, TILE - 1).astype(jnp.int32)
    object_field = gaussian(splits[3], (2, NY, NX), 1.0, 6.0, ((1, 8), (2, 16)), jnp.float32)
    probe = gaussian(splits[4], (2, P_SIZE, P_SIZE), 1.0, 6.0, (), jnp.float32)
    return dict(amplitudes=amplitudes, owners=owners, offsets=offsets, object_field=object_field, probe=probe)


def dft_tables(width, orient):
    steps_i = jnp.arange(width, dtype=jnp.int32)
    phase = steps_i[:, None] * steps_i[None, :] % width
    angles = phase.astype(jnp.float32) * (2.0 * math.pi / width)
    cos_table = (jnp.cos(angles) / math.sqrt(width)).astype(jnp.bfloat16)
    sin_table = (orient * jnp.sin(angles) / math.sqrt(width)).astype(jnp.bfloat16)
    col_table = jnp.concatenate([jnp.concatenate([cos_table, -sin_table], 1), jnp.concatenate([sin_table, cos_table], 1)], 0)
    return (cos_table, sin_table, col_table)

def transform(field_in, tables):
    cos_table, sin_table, col_table = tables
    width = cos_table.shape[0]
    direct = jnp.einsum('pk,bkm->bpm', cos_table.astype(jnp.float32), field_in.astype(jnp.float32))
    mixed = jnp.einsum('pk,bkm->bpm', sin_table.astype(jnp.float32), field_in.astype(jnp.float32))
    real_part = direct[..., :width] + mixed[..., width:]
    imag_part = direct[..., width:] - mixed[..., :width]
    halfway = jnp.concatenate([real_part, imag_part], -1).astype(jnp.bfloat16)
    return jnp.einsum('bpk,km->bpm', halfway.astype(jnp.float32), col_table.astype(jnp.float32))

def project(windows, amp_rows, live_mask, probe, forward, inverse):
    width = probe.shape[1]
    probe_re, probe_im = (probe[0], probe[1])
    obj_re, obj_im = (windows[:, 0], windows[:, 1])
    psi_re = probe_re * obj_re - probe_im * obj_im
    psi_im = probe_re * obj_im + probe_im * obj_re
    psi_b = jnp.concatenate([psi_re, psi_im], -1).astype(jnp.bfloat16)
    spectrum = transform(psi_b, forward)
    spec_re, spec_im = (spectrum[..., :width], spectrum[..., width:])
    ratio_mag = amp_rows.astype(jnp.float32) / jnp.sqrt(spec_re * spec_re + spec_im * spec_im + 0.01)
    projected = jnp.concatenate([spec_re * ratio_mag, spec_im * ratio_mag], -1).astype(jnp.bfloat16)
    revised = transform(projected, inverse)
    live_col = live_mask[:, None, None]
    diff_re = (revised[..., :width] - psi_re) * live_col
    diff_im = (revised[..., width:] - psi_im) * live_col
    obj_terms = jnp.stack([probe_re * diff_re + probe_im * diff_im, probe_re * diff_im - probe_im * diff_re, (probe_re * probe_re + probe_im * probe_im) * live_col], 1)
    probe_terms = jnp.stack([lax.optimization_barrier(jnp.sum(obj_re * diff_re + obj_im * diff_im, 0)), lax.optimization_barrier(jnp.sum(obj_re * diff_im - obj_im * diff_re, 0)), lax.optimization_barrier(jnp.sum((obj_re * obj_re + obj_im * obj_im) * live_col, 0))], 0)
    return (obj_terms, probe_terms)

def reference(amplitudes, owners, offsets, object_field, probe):
    forward = dft_tables(P_SIZE, 1.0)
    inverse = dft_tables(P_SIZE, -1.0)
    source = jnp.arange(PATTERNS, dtype=jnp.int32) // PAT_DEV
    row_start = jnp.minimum(source // N_TX * TILE + offsets[:, 0], NY - P_SIZE).astype(jnp.int32)
    col_start = jnp.minimum(owners[:, 0] * TILE + offsets[:, 1], NX - P_SIZE).astype(jnp.int32)
    blocks = PATTERNS // PAT_DEV
    amp_blocks = amplitudes.reshape(blocks, PAT_DEV, P_SIZE, P_SIZE)
    row_blocks = row_start.reshape(blocks, PAT_DEV)
    col_blocks = col_start.reshape(blocks, PAT_DEV)
    live_mask = jnp.ones((PAT_DEV,), jnp.float32)

    def advance(running, block_data):
        totals, probe_sums = running
        amp_rows, rows_here, cols_here = block_data
        windows = jax.vmap(lambda row_at, col_at: lax.dynamic_slice(object_field, (jnp.int32(0), row_at, col_at), (2, P_SIZE, P_SIZE)))(rows_here, cols_here)
        obj_terms, probe_terms = project(windows, amp_rows, live_mask, probe, forward, inverse)

        def deposit(entry, totals_now):
            corner = (jnp.int32(0), rows_here[entry], cols_here[entry])
            current = lax.dynamic_slice(totals_now, corner, (3, P_SIZE, P_SIZE))
            return lax.dynamic_update_slice(totals_now, current + obj_terms[entry], corner)
        totals = lax.fori_loop(0, PAT_DEV, deposit, totals)
        return ((totals, probe_sums + probe_terms), None)
    start_state = (jnp.zeros((3, NY, NX), jnp.float32), jnp.zeros((3, P_SIZE, P_SIZE), jnp.float32))
    (totals, probe_sums), _ = lax.scan(advance, start_state, (amp_blocks, row_blocks, col_blocks))
    object_new = object_field + totals[:2] / (totals[2] + 1.0)
    probe_step = probe_sums[:2] / jnp.sqrt(probe_sums[2] + 1.0)
    return (object_new, probe_step)
```

```python
import functools
import math

import jax
import jax.numpy as jnp
from jax import lax
from jax.experimental import pallas as pl
from jax.experimental.pallas import tpu as pltpu
from jax.sharding import PartitionSpec as P

W = 256
T = 512
SIDE = T + W
CAP = 3
RB = 32
LB = 128
MIB = 2**20


def shifted(value, axis, steps):
    count = lax.axis_size(axis)
    initial, last = (max(0, -steps), min(count, count - steps))
    return lax.ppermute(value, axis, [(source, source + steps) for source in range(initial, last)])


def tables():
    steps = jnp.arange(W, dtype=jnp.int32)
    phase = steps[:, None] * steps[None, :] % W
    angles = phase.astype(jnp.float32) * (2.0 * math.pi / W)
    c = (jnp.cos(angles) / math.sqrt(W)).astype(jnp.bfloat16)
    s = (jnp.sin(angles) / math.sqrt(W)).astype(jnp.bfloat16)
    ta = jnp.concatenate([jnp.concatenate([c, s], 1), jnp.concatenate([-s, c], 1)], 0)
    tb = jnp.concatenate([jnp.concatenate([c, -s], 1), jnp.concatenate([s, c], 1)], 0)
    return ta, tb


def pack_kernel(cols, owners, offsets, amp, packed, info, count, sem):
    n = amp.shape[0]
    rows_end = (lax.axis_size("ty") * T - W) - lax.axis_index("ty") * T
    for o in range(cols):
        count[o] = 0
        for k in range(4 * CAP):
            info[o, k] = 0

    def place(i, carry):
        o = owners[i, 0]
        k = count[o]
        count[o] = k + 1
        info[o, 4 * k] = jnp.minimum(offsets[i, 0], rows_end)
        info[o, 4 * k + 1] = jnp.minimum(offsets[i, 1], cols * T - W - o * T)
        info[o, 4 * k + 2] = 1
        pltpu.make_async_copy(amp.at[i], packed.at[k, o], sem.at[i]).start()
        return carry

    lax.fori_loop(0, n, place, 0)

    def finish(i, carry):
        pltpu.make_async_copy(amp.at[0], packed.at[0, 0], sem.at[i]).wait()
        return carry

    lax.fori_loop(0, n, finish, 0)


def pack(amp, owners, offsets):
    cols = lax.axis_size("tx")
    n = amp.shape[0]
    smem = pl.BlockSpec(memory_space=pltpu.SMEM)
    hbm = pl.BlockSpec(memory_space=pl.ANY)
    return pl.pallas_call(
        functools.partial(pack_kernel, cols),
        out_shape=(
            jax.ShapeDtypeStruct((CAP, cols, W, W), amp.dtype),
            jax.ShapeDtypeStruct((cols, 4 * CAP), jnp.int32),
        ),
        in_specs=[smem, smem, pl.BlockSpec(memory_space=pltpu.VMEM)],
        out_specs=(hbm, smem),
        scratch_shapes=[pltpu.SMEM((cols,), jnp.int32), pltpu.SemaphoreType.DMA((n,))],
        name="pack",
    )(owners, offsets, amp)


def chunk_kernel(slot, first, info, amp, obj, right, below, corner, probe, ta, tb, acc_in, ps_in, acc, ps, ext, win, xs, ys, sem):
    n = amp.shape[0]
    copies = []
    for p in range(2):
        for b in range(4):
            lanes = pl.ds(b * LB, LB)
            copies.append((obj.at[p, :, lanes], ext.at[p, b, pl.ds(0, T), :]))
            copies.append((below.at[p, :, lanes], ext.at[p, b, pl.ds(T, W), :]))
        for b in range(2):
            lanes = pl.ds(b * LB, LB)
            copies.append((right.at[p, :, lanes], ext.at[p, 4 + b, pl.ds(0, T), :]))
            copies.append((corner.at[p, :, lanes], ext.at[p, 4 + b, pl.ds(T, W), :]))
    if not first:
        copies.append((acc_in, acc))
        copies.append((ps_in, ps))
    copies = [pltpu.make_async_copy(a, b, sem.at[i]) for i, (a, b) in enumerate(copies)]
    for copy in copies:
        copy.start()
    if first:
        def clear(i, carry):
            for p in range(2):
                for b in range(6):
                    acc[p, b, pl.ds(i * RB, RB), :] = jnp.zeros((RB, LB), jnp.float32)
            return carry

        lax.fori_loop(0, SIDE // RB, clear, 0)
        ps[...] = jnp.zeros(ps.shape, jnp.float32)
    for copy in copies:
        copy.wait()
    lane = lax.broadcasted_iota(jnp.int32, (RB, LB), 1)

    def body(i, carry):
        r = info[i, 4 * slot]
        c = info[i, 4 * slot + 1]

        @pl.when(info[i, 4 * slot + 2] > 0)
        def _():
            cb = c // LB
            cs = c % LB
            back = (LB - cs) % LB
            low = lane < LB - cs
            high = lane >= cs
            for k in range(0, W, RB):
                o = []
                for p in range(2):
                    b = [pltpu.roll(ext[p, cb + j, pl.ds(r + k, RB), :], back, 1) for j in range(3)]
                    o.append([jnp.where(low, b[0], b[1]), jnp.where(low, b[1], b[2])])
                for h in range(2):
                    sl = slice(h * LB, h * LB + LB)
                    ore, oim = o[0][h], o[1][h]
                    win[0, k:k + RB, sl] = ore
                    win[1, k:k + RB, sl] = oim
                    pr, pi = probe[0, k:k + RB, sl], probe[1, k:k + RB, sl]
                    xs[k:k + RB, sl] = (pr * ore - pi * oim).astype(jnp.bfloat16)
                    xs[W + k:W + k + RB, sl] = (pr * oim + pi * ore).astype(jnp.bfloat16)
            y = jnp.dot(ta[...], xs[...], preferred_element_type=jnp.float32).astype(jnp.bfloat16)
            ys[:, :W] = y[:W]
            ys[:, W:] = y[W:]
            z = jnp.dot(ys[...], tb[...], preferred_element_type=jnp.float32)
            zr, zi = z[:, :W], z[:, W:]
            q = amp[i].astype(jnp.float32) * lax.rsqrt(zr * zr + zi * zi + 0.01)
            xs[:W] = (zr * q).astype(jnp.bfloat16)
            xs[W:] = (zi * q).astype(jnp.bfloat16)
            y = jnp.dot(tb[...], xs[...], preferred_element_type=jnp.float32).astype(jnp.bfloat16)
            ys[:, :W] = y[:W]
            ys[:, W:] = y[W:]
            z = jnp.dot(ys[...], ta[...], preferred_element_type=jnp.float32)
            for k in range(0, W, RB):
                t = [[], []]
                for h in range(2):
                    sl = slice(h * LB, h * LB + LB)
                    ore, oim = win[0, k:k + RB, sl], win[1, k:k + RB, sl]
                    pr, pi = probe[0, k:k + RB, sl], probe[1, k:k + RB, sl]
                    dr = z[k:k + RB, sl] - (pr * ore - pi * oim)
                    di = z[k:k + RB, W + h * LB:W + h * LB + LB] - (pr * oim + pi * ore)
                    t[0].append(pr * dr + pi * di)
                    t[1].append(pr * di - pi * dr)
                    ps[0, k:k + RB, sl] += ore * dr + oim * di
                    ps[1, k:k + RB, sl] += ore * di - oim * dr
                    ps[2, k:k + RB, sl] += ore * ore + oim * oim
                for p in range(2):
                    a = [pltpu.roll(t[p][h], cs, 1) for h in range(2)]
                    out = [jnp.where(high, a[0], 0.0), jnp.where(high, a[1], a[0]), jnp.where(high, 0.0, a[1])]
                    for j in range(3):
                        acc[p, cb + j, pl.ds(r + k, RB), :] += out[j]
        return carry

    lax.fori_loop(0, n, body, 0)


def chunk(slot, info, amp, obj, right, below, corner, probe, ta, tb, acc, ps):
    first = acc is None
    vm = pl.BlockSpec(memory_space=pltpu.VMEM)
    hbm = pl.BlockSpec(memory_space=pl.ANY)
    acc_shape = (2, SIDE // LB, SIDE, LB)
    ps_shape = (3, W, W)
    if first:
        acc = jnp.zeros((8, LB), jnp.float32)
        ps = acc
    return pl.pallas_call(
        functools.partial(chunk_kernel, slot, first),
        out_shape=(jax.ShapeDtypeStruct(acc_shape, jnp.float32), jax.ShapeDtypeStruct(ps_shape, jnp.float32)),
        in_specs=[pl.BlockSpec(memory_space=pltpu.SMEM), vm, hbm, hbm, hbm, hbm, vm, vm, vm, hbm, hbm],
        out_specs=(vm, vm),
        scratch_shapes=[
            pltpu.VMEM((2, SIDE // LB, SIDE, LB), jnp.float32),
            pltpu.VMEM((2, W, W), jnp.float32),
            pltpu.VMEM((2 * W, W), jnp.bfloat16),
            pltpu.VMEM((W, 2 * W), jnp.bfloat16),
            pltpu.SemaphoreType.DMA((26,)),
        ],
        compiler_params=pltpu.CompilerParams(vmem_limit_bytes=50 * MIB),
        cost_estimate=pl.CostEstimate(flops=16 * 540_000_000, bytes_accessed=40_000_000, transcendentals=16 * W * W),
        name="project_slot",
    )(info, amp, obj, right, below, corner, probe, ta, tb, acc, ps)


def den_kernel(info, probe, den, pp):
    def clear(i, carry):
        for b in range(SIDE // LB):
            den[b, pl.ds(i * RB, RB), :] = jnp.zeros((RB, LB), jnp.float32)
        return carry

    lax.fori_loop(0, SIDE // RB, clear, 0)
    for h in range(2):
        lanes = slice(h * LB, h * LB + LB)
        pp[h] = probe[0, :, lanes] * probe[0, :, lanes] + probe[1, :, lanes] * probe[1, :, lanes]
    lane = lax.broadcasted_iota(jnp.int32, (RB, LB), 1)

    for slot in range(CAP):
        def body(i, carry):
            r = info[i, 4 * slot]
            c = info[i, 4 * slot + 1]

            @pl.when(info[i, 4 * slot + 2] > 0)
            def _():
                cb = c // LB
                cs = c % LB
                high = lane >= cs
                for k in range(0, W, RB):
                    a = [pltpu.roll(pp[h, k:k + RB, :], cs, 1) for h in range(2)]
                    out = [jnp.where(high, a[0], 0.0), jnp.where(high, a[1], a[0]), jnp.where(high, 0.0, a[1])]
                    for j in range(3):
                        den[cb + j, pl.ds(r + k, RB), :] += out[j]

            return carry

        lax.fori_loop(0, info.shape[0], body, 0)


def denominator(info, probe):
    vm = pl.BlockSpec(memory_space=pltpu.VMEM)
    return pl.pallas_call(
        den_kernel,
        out_shape=jax.ShapeDtypeStruct((SIDE // LB, SIDE, LB), jnp.float32),
        in_specs=[pl.BlockSpec(memory_space=pltpu.SMEM), vm],
        out_specs=vm,
        scratch_shapes=[pltpu.VMEM((2, W, LB), jnp.float32)],
        compiler_params=pltpu.CompilerParams(vmem_limit_bytes=16 * MIB),
        cost_estimate=pl.CostEstimate(flops=40_000_000, bytes_accessed=3_000_000, transcendentals=0),
        name="denominator",
    )(info, probe)


def tail_kernel(
    acc, ps, den, den_right, den_below, den_corner, obj, out, step,
    s_right, s_below, s_corner, g_right, g_below, g_corner, inv, ra, sb, rb, gc, gd,
    sa, qa, sbs, qb, scs, qc, sds, qd, ses, qe,
):
    ny, nx = lax.axis_size("ty"), lax.axis_size("tx")
    ty, tx = lax.axis_index("ty"), lax.axis_index("tx")
    barrier = pltpu.get_barrier_semaphore()
    down, up = lax.rem(ty + 1, ny), lax.rem(ty + ny - 1, ny)
    east, west = lax.rem(tx + 1, nx), lax.rem(tx + nx - 1, nx)
    greet = [(lax.rem(ty + d, ny), tx) for d in range(1, ny)] + [(ty, lax.rem(tx + d, nx)) for d in range(1, nx)]
    greet += [(down, east), (up, west)]
    for other in greet:
        pl.semaphore_signal(barrier, inc=1, device_id=other, device_id_type=pl.DeviceIdType.MESH)

    for p in range(2):
        for b in range(2):
            s_right[p, b] = acc[p, 4 + b, :T, :].astype(jnp.bfloat16)
            s_corner[p, b] = acc[p, 4 + b, T:, :].astype(jnp.bfloat16)
        for b in range(4):
            s_below[p, b] = acc[p, b, T:, :].astype(jnp.bfloat16)
    pl.semaphore_wait(barrier, len(greet))

    def send(src, dst, s, q, device):
        copy = pltpu.make_async_remote_copy(
            src_ref=src, dst_ref=dst, send_sem=s, recv_sem=q, device_id=device, device_id_type=pl.DeviceIdType.MESH
        )
        copy.start()
        return copy

    rows = W // ny
    stage_a = []
    for d in range(1, ny):
        peer = lax.rem(ty + d, ny)
        stage_a.append(
            send(ps.at[:, pl.ds(pl.multiple_of(peer * rows, rows), rows), :], ra.at[ty], sa.at[d - 1], qa.at[d - 1], (peer, tx))
        )
    strips = [
        send(s_right, g_right, ses.at[0], qe.at[0], (ty, east)),
        send(s_corner, g_corner, ses.at[1], qe.at[1], (down, east)),
        send(s_below, g_below, ses.at[2], qe.at[2], (down, tx)),
    ]
    ra[ty] = ps[:, pl.ds(pl.multiple_of(ty * rows, rows), rows), :]

    for b in range(4):
        total = den[b, :T, :]
        if b < 2:
            total = total + den_right[b]
        low = den_below[b]
        if b < 2:
            low = low + den_corner[b]
        inv[b, :W, :] = 1.0 / (total[:W] + low + 1.0)
        inv[b, W:, :] = 1.0 / (total[W:] + 1.0)

    for copy in stage_a:
        copy.wait_recv()
    total = ra[0]
    for j in range(1, ny):
        total = total + ra[j]
    for j in range(nx):
        p, g, h = j // (nx // 2), j // 2 % (rows // 8), j % 2
        lanes = slice(h * LB, h * LB + LB)
        sb[j, 0] = total[p, g * 8:g * 8 + 8, lanes]
        sb[j, 1] = total[2, g * 8:g * 8 + 8, lanes]
    stage_b = []
    for d in range(1, nx):
        peer = lax.rem(tx + d, nx)
        stage_b.append(send(sb.at[peer], rb.at[tx], sbs.at[d - 1], qb.at[d - 1], (ty, peer)))
    rb[tx] = sb[tx]
    for copy in stage_b:
        copy.wait_recv()
    total = rb[0]
    for j in range(1, nx):
        total = total + rb[j]
    gc[tx] = total[0] / jnp.sqrt(total[1] + 1.0)
    stage_c = []
    for d in range(1, nx):
        peer = lax.rem(tx + d, nx)
        stage_c.append(send(gc.at[tx], gc.at[tx], scs.at[d - 1], qc.at[d - 1], (ty, peer)))
    for copy in stage_c:
        copy.wait_recv()
    gd[ty] = gc[...]
    stage_d = []
    for d in range(1, ny):
        peer = lax.rem(ty + d, ny)
        stage_d.append(send(gc, gd.at[ty], sds.at[d - 1], qd.at[d - 1], (peer, tx)))

    for copy in strips:
        copy.wait_recv()
    has_west = jnp.where(tx > 0, 1.0, 0.0)
    has_north = jnp.where(ty > 0, 1.0, 0.0)
    has_both = has_west * has_north

    def upper(i, carry):
        at = pl.ds(pl.multiple_of(i * RB, RB), RB)
        for b in range(4):
            lanes = slice(b * LB, b * LB + LB)
            for p in range(2):
                num = acc[p, b, at, :] + has_north * g_below[p, b, at, :].astype(jnp.float32)
                if b < 2:
                    num = num + has_west * g_right[p, b, at, :].astype(jnp.float32)
                    num = num + has_both * g_corner[p, b, at, :].astype(jnp.float32)
                out[p, at, lanes] = obj[p, at, lanes] + num * inv[b, at, :]
        return carry

    def lower(i, carry):
        at = pl.ds(pl.multiple_of(i * RB, RB), RB)
        for b in range(4):
            lanes = slice(b * LB, b * LB + LB)
            for p in range(2):
                num = acc[p, b, at, :]
                if b < 2:
                    num = num + has_west * g_right[p, b, at, :].astype(jnp.float32)
                out[p, at, lanes] = obj[p, at, lanes] + num * inv[b, at, :]
        return carry

    lax.fori_loop(0, W // RB, upper, 0)
    lax.fori_loop(W // RB, T // RB, lower, 0)

    for copy in stage_d:
        copy.wait_recv()
    for t in range(ny):
        for j in range(nx):
            p, g, h = j // (nx // 2), j // 2 % (rows // 8), j % 2
            step[p, t * rows + g * 8:t * rows + g * 8 + 8, h * LB:h * LB + LB] = gd[t, j]
    for copy in stage_a + strips + stage_b + stage_c + stage_d:
        copy.wait_send()


def tail(acc, ps, den, den_right, den_below, den_corner, obj):
    ny, nx = lax.axis_size("ty"), lax.axis_size("tx")
    vm = pl.BlockSpec(memory_space=pltpu.VMEM)
    bf, f32 = jnp.bfloat16, jnp.float32
    dma = pltpu.SemaphoreType.DMA
    strips = [(2, 2, T, LB), (2, 4, W, LB), (2, 2, W, LB)]
    return pl.pallas_call(
        tail_kernel,
        out_shape=(jax.ShapeDtypeStruct(obj.shape, f32), jax.ShapeDtypeStruct((2, W, W), f32)),
        in_specs=[vm] * 7,
        out_specs=(vm, vm),
        scratch_shapes=[pltpu.VMEM(x, bf) for x in strips + strips]
        + [
            pltpu.VMEM((4, T, LB), f32),
            pltpu.VMEM((ny, 3, W // ny, W), f32),
            pltpu.VMEM((nx, 2, 8, LB), f32),
            pltpu.VMEM((nx, 2, 8, LB), f32),
            pltpu.VMEM((nx, 8, LB), f32),
            pltpu.VMEM((ny, nx, 8, LB), f32),
        ]
        + [dma((k,)) for k in (ny - 1, ny - 1, nx - 1, nx - 1, nx - 1, nx - 1, ny - 1, ny - 1, 3, 3)],
        compiler_params=pltpu.CompilerParams(vmem_limit_bytes=50 * MIB, collective_id=0, has_side_effects=True),
        name="exchange",
    )(acc, ps, den, den_right, den_below, den_corner, obj)


def local(amplitudes, owners, offsets, object_field, probe):
    right = shifted(object_field[:, :, :W], "tx", -1)
    below = shifted(object_field[:, :W, :], "ty", -1)
    corner = shifted(right[:, :W, :], "ty", -1)
    packed, info = pack(amplitudes, owners, offsets)
    got_info = lax.all_to_all(info, "tx", split_axis=0, concat_axis=0, tiled=True)
    den = denominator(got_info, probe)
    den_right = shifted(den[4:, :T], "tx", 1)
    den_below = shifted(den[:, T:], "ty", 1)
    den_corner = shifted(den_below[4:], "tx", 1)
    ta, tb = tables()
    acc, ps = None, None
    for slot in range(CAP):
        got = lax.all_to_all(packed[slot], "tx", split_axis=0, concat_axis=0, tiled=True)
        acc, ps = chunk(slot, got_info, got, object_field, right, below, corner, probe, ta, tb, acc, ps)
    return tail(acc, ps, den, den_right, den_below, den_corner, object_field)


def solution(mesh):
    return jax.shard_map(
        local,
        mesh=mesh,
        in_specs=(
            P(("ty", "tx"), None, None),
            P(("ty", "tx"), None),
            P(("ty", "tx"), None),
            P(None, "ty", "tx"),
            P(),
        ),
        out_specs=(P(None, "ty", "tx"), P()),
        check_vma=False,
    )
```

```python
import functools
import math

import jax
import jax.numpy as jnp
from jax import lax
from jax.experimental import pallas as pl
from jax.experimental.pallas import tpu as pltpu
from jax.sharding import PartitionSpec as P

W = 256
T = 512
SIDE = T + W
CAP = 3
PATS = 32
GROUP = 3
CH = 64
FRAME = W + 2 * CH
RB = 32
LB = 128
MIB = 2**20


def tables():
    steps = jnp.arange(W, dtype=jnp.int32)
    phase = steps[:, None] * steps[None, :] % W
    angles = phase.astype(jnp.float32) * (2.0 * math.pi / W)
    c = (jnp.cos(angles) / math.sqrt(W)).astype(jnp.bfloat16)
    s = (jnp.sin(angles) / math.sqrt(W)).astype(jnp.bfloat16)
    ta = jnp.concatenate([jnp.concatenate([c, s], 1), jnp.concatenate([-s, c], 1)], 0)
    tb = jnp.concatenate([jnp.concatenate([c, -s], 1), jnp.concatenate([s, c], 1)], 0)
    return ta, tb


def plan_kernel(meta, plan):
    ny, nx = lax.axis_size("ty"), lax.axis_size("tx")
    ty = lax.axis_index("ty")
    owner, row, col = meta[0:1, :], meta[1:2, :], meta[2:3, :]
    lane1 = lax.broadcasted_iota(jnp.int32, (1, LB), 1)
    rank = jnp.zeros((1, LB), jnp.int32)
    for d in range(1, PATS):
        rank = rank + jnp.where((pltpu.roll(owner, d, 1) == owner) & (lane1 >= d), 1, 0)
    target = jnp.where(lane1 < PATS, owner * 8 + rank, -1)
    row = jnp.minimum(row, ny * T - W - ty * T).astype(jnp.float32)
    col = jnp.minimum(col, nx * T - W - owner * T).astype(jnp.float32)
    one = jnp.ones((1, LB), jnp.float32)
    lane8 = lax.broadcasted_iota(jnp.int32, (8, LB), 1)
    sub8 = lax.broadcasted_iota(jnp.int32, (8, LB), 0)
    for o in range(nx):
        hit = (sub8 + 8 * o) == target
        tile = jnp.zeros((8, LB), jnp.float32)
        for f, field in enumerate((row, col, one, lane1.astype(jnp.float32))):
            value = jnp.sum(jnp.where(hit, field, 0.0), axis=1, keepdims=True)
            tile = jnp.where(lane8 == f, value, tile)
        plan[o] = tile.astype(jnp.int32)


def plan_of(owners, offsets):
    vm = pl.BlockSpec(memory_space=pltpu.VMEM)
    meta = jnp.pad(jnp.concatenate([owners, offsets], 1).T, ((0, 5), (0, LB - PATS)))
    return pl.pallas_call(
        plan_kernel,
        out_shape=jax.ShapeDtypeStruct((lax.axis_size("tx"), 8, LB), jnp.int32),
        in_specs=[vm],
        out_specs=vm,
        name="plan",
    )(meta)


def mesh_copy(src, dst, s, q, device):
    return pltpu.make_async_remote_copy(
        src_ref=src, dst_ref=dst, send_sem=s, recv_sem=q, device_id=device, device_id_type=pl.DeviceIdType.MESH
    )


def dot(a, b):
    return jnp.dot(a, b, preferred_element_type=jnp.float32)


def update_kernel(
    plan, amp, obj, probe, ta, tb, out, step,
    ext, sbuf, rbuf, ginfo, planm, infom, tpad, den, acc, ps, inv, win, xs, ys,
    d_right, d_below, d_corner, s_right, s_below, s_corner, g_right, g_below, g_corner, ra, sb, rb, gc, gd,
    si, qi, sp, qp, sh, qh, sc, qc, sd, qd, sa, qa, sbs, qb, scs, qcs, sds, qds, ses, qes, sl,
):
    ny, nx = lax.axis_size("ty"), lax.axis_size("tx")
    ty, tx = lax.axis_index("ty"), lax.axis_index("tx")
    down, up = lax.rem(ty + 1, ny), lax.rem(ty + ny - 1, ny)
    east, west = lax.rem(tx + 1, nx), lax.rem(tx + nx - 1, nx)
    barrier = pltpu.get_barrier_semaphore()
    greet = [(ty, lax.rem(tx + d, nx)) for d in range(1, nx)] + [(lax.rem(ty + d, ny), tx) for d in range(1, ny)]
    greet += [(up, west), (down, east)]
    for other in greet:
        pl.semaphore_signal(barrier, inc=1, device_id=other, device_id_type=pl.DeviceIdType.MESH)

    own = []
    for p in range(2):
        for b in range(4):
            own.append(pltpu.make_async_copy(obj.at[p, :, pl.ds(b * LB, LB)], ext.at[p, b, pl.ds(0, T), :], sl.at[len(own)]))
    for copy in own:
        copy.start()
    to_smem = pltpu.make_async_copy(plan, planm, sl.at[8])
    to_smem.start()

    def partner(i, sign):
        d = lax.rem(7 * i, nx)
        y, z = tx // 4, lax.rem(tx, 4)
        dy, dz = d // 4, lax.rem(d, 4)
        return lax.rem(y + nx + sign * dy, nx // 4) * 4 + lax.rem(z + 4 + sign * dz, 4)

    def info_copy(i):
        peer = partner(i, 1)
        return mesh_copy(plan.at[peer], ginfo.at[i], si.at[i - 1], qi.at[i - 1], (ty, peer))

    def amp_copy(m):
        return mesh_copy(sbuf.at[m], rbuf.at[m], sp.at[m], qp.at[m], (ty, partner(lax.rem(m, nx), 1)))

    halo, below = [], []
    for p in range(2):
        for b in range(2):
            k, lanes = len(halo), pl.ds(b * LB, LB)
            halo.append(mesh_copy(obj.at[p, :, lanes], ext.at[p, 4 + b, pl.ds(0, T), :], sh.at[k], qh.at[k], (ty, west)))
    for p in range(2):
        for b in range(4):
            k, lanes = 4 + len(below), pl.ds(b * LB, LB)
            below.append(mesh_copy(obj.at[p, pl.ds(0, W), lanes], ext.at[p, b, pl.ds(T, W), :], sh.at[k], qh.at[k], (up, tx)))

    pl.semaphore_wait(barrier, len(greet))
    lax.fori_loop(1, nx, lambda i, c: (info_copy(i).start(), c)[1], 0)
    for copy in halo + below:
        copy.start()
    ginfo[0] = plan[tx]
    to_smem.wait()

    def pack(m, carry):
        i, k = lax.rem(m, nx), m // nx

        @pl.when(i > 0)
        def _():
            sbuf[m] = amp[planm[partner(i, 1), k, 3]]
            amp_copy(m).start()

        @pl.when(i == 0)
        def _():
            rbuf[m] = amp[planm[tx, k, 3]]

        return carry

    lax.fori_loop(0, CAP * nx, pack, 0)

    for q in range(GROUP):
        for p in range(2):
            for b in range(5):
                tpad[q, p, b] = jnp.zeros((FRAME, LB), jnp.float32)

    def clear(i, carry):
        at = pl.ds(pl.multiple_of(i * CH, CH), CH)
        zero = jnp.zeros((CH, LB), jnp.float32)
        for b in range(SIDE // LB):
            den[b, at, :] = zero
            for p in range(2):
                acc[p, b, at, :] = zero
        return carry

    lax.fori_loop(0, SIDE // CH, clear, 0)
    ps[...] = jnp.zeros(ps.shape, jnp.float32)
    lax.fori_loop(1, nx, lambda i, c: (info_copy(i).wait_recv(), c)[1], 0)
    to_smem = pltpu.make_async_copy(ginfo, infom, sl.at[8])
    to_smem.start()
    to_smem.wait()
    lane = lax.broadcasted_iota(jnp.int32, (RB, LB), 1)

    def windows(g):
        found = []
        for q in range(GROUP):
            m = g * GROUP + q
            i, k = lax.rem(m, nx), m // nx
            found.append((infom[i, k, 0], infom[i, k, 1], infom[i, k, 2].astype(jnp.float32)))
        return found

    def place(q, p, k, halves, cs):
        high = lane >= cs
        a = [pltpu.roll(half, cs, 1) for half in halves]
        at = slice(CH + k, CH + k + RB)
        tpad[q, p, 1, at, :] = jnp.where(high, a[0], 0.0)
        tpad[q, p, 2, at, :] = jnp.where(high, a[1], a[0])
        tpad[q, p, 3, at, :] = jnp.where(high, 0.0, a[1])

    def pull(found, planes):
        cols = [[jnp.clip(b - c // LB, -1, 3) + 1 for b in range(SIDE // LB)] for _, c, _ in found]

        def rows(j, carry):
            y0 = pl.multiple_of(j * CH, CH)
            starts = [jnp.clip(y0 - r, -CH, W) + CH for r, _, _ in found]
            for b in range(SIDE // LB):
                for p, ref in enumerate(planes):
                    v = ref[b, pl.ds(y0, CH), :]
                    for q in range(GROUP):
                        v = v + tpad[q, p, cols[q][b], pl.ds(starts[q], CH), :]
                    ref[b, pl.ds(y0, CH), :] = v
            return carry

        lax.fori_loop(0, SIDE // CH, rows, 0)

    def spread(g, carry):
        found = windows(g)
        for k in range(0, W, RB):
            power = []
            for h in range(2):
                at = slice(h * LB, h * LB + LB)
                pr, pi = probe[0, k:k + RB, at], probe[1, k:k + RB, at]
                power.append(pr * pr + pi * pi)
            for q in range(GROUP):
                place(q, 0, k, [x * found[q][2] for x in power], lax.rem(found[q][1], LB))
        pull(found, [den])
        return carry

    groups = CAP * nx // GROUP
    lax.fori_loop(0, groups, spread, 0)
    d_strips = [
        mesh_copy(den.at[pl.ds(4, 2), pl.ds(0, T), :], d_right, sd.at[0], qd.at[0], (ty, east)),
        mesh_copy(den.at[pl.ds(4, 2), pl.ds(T, W), :], d_corner, sd.at[1], qd.at[1], (down, east)),
        mesh_copy(den.at[pl.ds(0, 4), pl.ds(T, W), :], d_below, sd.at[2], qd.at[2], (down, tx)),
    ]
    for copy in d_strips:
        copy.start()

    for copy in halo:
        copy.wait_recv()
    corner = []
    for p in range(2):
        strip = ext.at[p, pl.ds(4, 2), pl.ds(0, W), :]
        corner.append(mesh_copy(strip, ext.at[p, pl.ds(4, 2), pl.ds(T, W), :], sc.at[p], qc.at[p], (up, tx)))
    for copy in corner:
        copy.start()
    for copy in own:
        copy.wait()
    for copy in below + corner:
        copy.wait_recv()

    def half(t, q):
        y = dot(t[...], xs[q]).astype(jnp.bfloat16)
        ys[q, :, :W] = y[:W]
        ys[q, :, W:] = y[W:]

    def group(g, carry):
        found = windows(g)
        for q in range(GROUP):
            m = g * GROUP + q

            @pl.when(lax.rem(m, nx) > 0)
            def _():
                amp_copy(m).wait_recv()

        for q in range(GROUP):
            r, c, _ = found[q]
            cb, cs = c // LB, lax.rem(c, LB)
            back = lax.rem(LB - cs, LB)
            low = lane < LB - cs
            for k in range(0, W, RB):
                o = []
                for p in range(2):
                    b = [pltpu.roll(ext[p, cb + j, pl.ds(r + k, RB), :], back, 1) for j in range(3)]
                    o.append([jnp.where(low, b[0], b[1]), jnp.where(low, b[1], b[2])])
                for h in range(2):
                    at = slice(h * LB, h * LB + LB)
                    ore, oim = o[0][h], o[1][h]
                    win[q, 0, k:k + RB, at] = ore
                    win[q, 1, k:k + RB, at] = oim
                    pr, pi = probe[0, k:k + RB, at], probe[1, k:k + RB, at]
                    xs[q, k:k + RB, at] = (pr * ore - pi * oim).astype(jnp.bfloat16)
                    xs[q, W + k:W + k + RB, at] = (pr * oim + pi * ore).astype(jnp.bfloat16)
        for q in range(GROUP):
            half(ta, q)
        for q in range(GROUP):
            z = dot(ys[q], tb[...])
            zr, zi = z[:, :W], z[:, W:]
            f = rbuf[g * GROUP + q].astype(jnp.float32) * lax.rsqrt(zr * zr + zi * zi + 0.01)
            xs[q, :W] = (zr * f).astype(jnp.bfloat16)
            xs[q, W:] = (zi * f).astype(jnp.bfloat16)
        for q in range(GROUP):
            half(tb, q)
        zs = [dot(ys[q], ta[...]) for q in range(GROUP)]
        for k in range(0, W, RB):
            terms = [[[], []] for q in range(GROUP)]
            for h in range(2):
                at = slice(h * LB, h * LB + LB)
                pr, pi = probe[0, k:k + RB, at], probe[1, k:k + RB, at]
                sums = None
                for q in range(GROUP):
                    live = found[q][2]
                    ore, oim = win[q, 0, k:k + RB, at], win[q, 1, k:k + RB, at]
                    dr = (zs[q][k:k + RB, at] - (pr * ore - pi * oim)) * live
                    di = (zs[q][k:k + RB, W + h * LB:W + h * LB + LB] - (pr * oim + pi * ore)) * live
                    terms[q][0].append(pr * dr + pi * di)
                    terms[q][1].append(pr * di - pi * dr)
                    mine = (ore * dr + oim * di, ore * di - oim * dr, (ore * ore + oim * oim) * live)
                    sums = mine if sums is None else tuple(x + y for x, y in zip(sums, mine))
                for j in range(3):
                    ps[j, k:k + RB, at] += sums[j]
            for q in range(GROUP):
                for p in range(2):
                    place(q, p, k, terms[q][p], lax.rem(found[q][1], LB))
        pull(found, [acc.at[0], acc.at[1]])
        return carry

    lax.fori_loop(0, groups, group, 0)

    def send(*args):
        copy = mesh_copy(*args)
        copy.start()
        return copy

    rows = W // ny
    stage_a = []
    for d in range(1, ny):
        peer = lax.rem(ty + d, ny)
        piece = ps.at[:, pl.ds(pl.multiple_of(peer * rows, rows), rows), :]
        stage_a.append(send(piece, ra.at[ty], sa.at[d - 1], qa.at[d - 1], (peer, tx)))
    for p in range(2):
        for b in range(2):
            s_right[p, b] = acc[p, 4 + b, :T, :].astype(jnp.bfloat16)
    strips = [send(s_right, g_right, ses.at[0], qes.at[0], (ty, east))]
    for p in range(2):
        for b in range(2):
            s_corner[p, b] = acc[p, 4 + b, T:, :].astype(jnp.bfloat16)
    strips.append(send(s_corner, g_corner, ses.at[1], qes.at[1], (down, east)))
    for p in range(2):
        for b in range(4):
            s_below[p, b] = acc[p, b, T:, :].astype(jnp.bfloat16)
    strips.append(send(s_below, g_below, ses.at[2], qes.at[2], (down, tx)))
    ra[ty] = ps[:, pl.ds(pl.multiple_of(ty * rows, rows), rows), :]

    for copy in d_strips:
        copy.wait_recv()
    has_west = jnp.where(tx > 0, 1.0, 0.0)
    has_north = jnp.where(ty > 0, 1.0, 0.0)
    has_both = has_west * has_north
    for b in range(4):
        top, rest = den[b, :W, :] + has_north * d_below[b], den[b, W:T, :]
        if b < 2:
            top = top + (has_west * d_right[b, :W, :] + has_both * d_corner[b])
            rest = rest + has_west * d_right[b, W:, :]
        inv[b, :W, :] = 1.0 / (top + 1.0)
        inv[b, W:, :] = 1.0 / (rest + 1.0)

    for copy in stage_a:
        copy.wait_recv()
    total = ra[0]
    for j in range(1, ny):
        total = total + ra[j]
    for j in range(nx):
        p, g, h = j // (nx // 2), j // 2 % (rows // 8), j % 2
        lanes = slice(h * LB, h * LB + LB)
        sb[j, 0] = total[p, g * 8:g * 8 + 8, lanes]
        sb[j, 1] = total[2, g * 8:g * 8 + 8, lanes]
    stage_b = []
    for d in range(1, nx):
        peer = lax.rem(tx + d, nx)
        stage_b.append(send(sb.at[peer], rb.at[tx], sbs.at[d - 1], qb.at[d - 1], (ty, peer)))
    rb[tx] = sb[tx]
    for copy in stage_b:
        copy.wait_recv()
    total = rb[0]
    for j in range(1, nx):
        total = total + rb[j]
    gc[tx] = total[0] / jnp.sqrt(total[1] + 1.0)
    stage_c = []
    for d in range(1, nx):
        peer = lax.rem(tx + d, nx)
        stage_c.append(send(gc.at[tx], gc.at[tx], scs.at[d - 1], qcs.at[d - 1], (ty, peer)))
    for copy in stage_c:
        copy.wait_recv()
    gd[ty] = gc[...]
    stage_d = []
    for d in range(1, ny):
        peer = lax.rem(ty + d, ny)
        stage_d.append(send(gc, gd.at[ty], sds.at[d - 1], qds.at[d - 1], (peer, tx)))

    for copy in strips:
        copy.wait_recv()

    def upper(i, carry):
        at = pl.ds(pl.multiple_of(i * RB, RB), RB)
        for b in range(4):
            lanes = slice(b * LB, b * LB + LB)
            for p in range(2):
                num = acc[p, b, at, :] + has_north * g_below[p, b, at, :].astype(jnp.float32)
                if b < 2:
                    num = num + has_west * g_right[p, b, at, :].astype(jnp.float32)
                    num = num + has_both * g_corner[p, b, at, :].astype(jnp.float32)
                out[p, at, lanes] = ext[p, b, at, :] + num * inv[b, at, :]
        return carry

    def lower(i, carry):
        at = pl.ds(pl.multiple_of(i * RB, RB), RB)
        for b in range(4):
            lanes = slice(b * LB, b * LB + LB)
            for p in range(2):
                num = acc[p, b, at, :]
                if b < 2:
                    num = num + has_west * g_right[p, b, at, :].astype(jnp.float32)
                out[p, at, lanes] = ext[p, b, at, :] + num * inv[b, at, :]
        return carry

    lax.fori_loop(0, W // RB, upper, 0)
    lax.fori_loop(W // RB, T // RB, lower, 0)

    for copy in stage_d:
        copy.wait_recv()
    for t in range(ny):
        for j in range(nx):
            p, g, h = j // (nx // 2), j // 2 % (rows // 8), j % 2
            step[p, t * rows + g * 8:t * rows + g * 8 + 8, h * LB:h * LB + LB] = gd[t, j]
    for copy in halo + below + corner + d_strips + stage_a + strips + stage_b + stage_c + stage_d:
        copy.wait_send()
    lax.fori_loop(1, nx, lambda i, c: (info_copy(i).wait_send(), c)[1], 0)

    def sent(m, carry):
        @pl.when(lax.rem(m, nx) > 0)
        def _():
            amp_copy(m).wait_send()

        return carry

    lax.fori_loop(0, CAP * nx, sent, 0)


def update(plan, amp, obj, probe, ta, tb):
    ny, nx = lax.axis_size("ty"), lax.axis_size("tx")
    vm = pl.BlockSpec(memory_space=pltpu.VMEM)
    bf, f32, i32 = jnp.bfloat16, jnp.float32, jnp.int32
    dma = pltpu.SemaphoreType.DMA
    blocks = SIDE // LB
    strips = [(2, 2, T, LB), (2, 4, W, LB), (2, 2, W, LB)]
    sems = [nx - 1, nx - 1, CAP * nx, CAP * nx, 12, 12, 2, 2, 3, 3]
    sems += [ny - 1, ny - 1, nx - 1, nx - 1, nx - 1, nx - 1, ny - 1, ny - 1, 3, 3, 9]
    return pl.pallas_call(
        update_kernel,
        out_shape=(jax.ShapeDtypeStruct(obj.shape, f32), jax.ShapeDtypeStruct((2, W, W), f32)),
        in_specs=[vm, vm, pl.BlockSpec(memory_space=pl.ANY), vm, vm, vm],
        out_specs=(vm, vm),
        scratch_shapes=[
            pltpu.VMEM((2, blocks, SIDE, LB), f32),
            pltpu.VMEM((CAP * nx, W, W), bf),
            pltpu.VMEM((CAP * nx, W, W), bf),
            pltpu.VMEM((nx, 8, LB), i32),
            pltpu.SMEM((nx, 8, LB), i32),
            pltpu.SMEM((nx, 8, LB), i32),
            pltpu.VMEM((GROUP, 2, 5, FRAME, LB), f32),
            pltpu.VMEM((blocks, SIDE, LB), f32),
            pltpu.VMEM((2, blocks, SIDE, LB), f32),
            pltpu.VMEM((3, W, W), f32),
            pltpu.VMEM((4, T, LB), f32),
            pltpu.VMEM((GROUP, 2, W, W), f32),
            pltpu.VMEM((GROUP, 2 * W, W), bf),
            pltpu.VMEM((GROUP, W, 2 * W), bf),
        ]
        + [pltpu.VMEM(x[1:], f32) for x in strips]
        + [pltpu.VMEM(x, bf) for x in strips + strips]
        + [
            pltpu.VMEM((ny, 3, W // ny, W), f32),
            pltpu.VMEM((nx, 2, 8, LB), f32),
            pltpu.VMEM((nx, 2, 8, LB), f32),
            pltpu.VMEM((nx, 8, LB), f32),
            pltpu.VMEM((ny, nx, 8, LB), f32),
        ]
        + [dma((k,)) for k in sems],
        compiler_params=pltpu.CompilerParams(vmem_limit_bytes=60 * MIB, collective_id=0, has_side_effects=True),
        name="update",
    )(plan, amp, obj, probe, ta, tb)


def local(amplitudes, owners, offsets, object_field, probe):
    plan = plan_of(owners, offsets)
    ta, tb = tables()
    return update(plan, amplitudes, object_field, probe, ta, tb)


def solution(mesh):
    return jax.shard_map(
        local,
        mesh=mesh,
        in_specs=(
            P(("ty", "tx"), None, None),
            P(("ty", "tx"), None),
            P(("ty", "tx"), None),
            P(None, "ty", "tx"),
            P(),
        ),
        out_specs=(P(None, "ty", "tx"), P()),
        check_vma=False,
    )
```

```python
import functools
import math

import jax
import jax.numpy as jnp
import ml_dtypes
import numpy as np
from jax import lax
from jax.experimental import pallas as pl
from jax.experimental.pallas import tpu as pltpu
from jax.sharding import PartitionSpec as P

W = 256
T = 512
SIDE = T + W
CAP = 3
PATS = 32
GROUP = 3
FIRST = 16
AHEAD = 3
CH = 64
FRAME = W + 2 * CH
RB = 32
LB = 128
MIB = 2**20


def tables():
    steps = np.arange(W)
    phase = (steps[:, None] * steps[None, :] % W).astype(np.float32)
    angles = phase * np.float32(2.0 * math.pi / W)
    c, s = np.cos(angles) / np.float32(math.sqrt(W)), np.sin(angles) / np.float32(math.sqrt(W))
    ta, tb = np.block([[c, s], [-s, c]]), np.block([[c, -s], [s, c]])
    return jnp.asarray(ta.astype(ml_dtypes.bfloat16)), jnp.asarray(tb.astype(ml_dtypes.bfloat16))


def plan_kernel(meta, plan):
    ny, nx = lax.axis_size("ty"), lax.axis_size("tx")
    ty = lax.axis_index("ty")
    owner, row, col = meta[0:1, :], meta[1:2, :], meta[2:3, :]
    lane1 = lax.broadcasted_iota(jnp.int32, (1, LB), 1)
    rank = jnp.zeros((1, LB), jnp.int32)
    for d in range(1, PATS):
        rank = rank + jnp.where((pltpu.roll(owner, d, 1) == owner) & (lane1 >= d), 1, 0)
    target = jnp.where(lane1 < PATS, owner * 8 + rank, -1)
    row = jnp.minimum(row, ny * T - W - ty * T).astype(jnp.float32)
    col = jnp.minimum(col, nx * T - W - owner * T).astype(jnp.float32)
    one = jnp.ones((1, LB), jnp.float32)
    lane8 = lax.broadcasted_iota(jnp.int32, (8, LB), 1)
    sub8 = lax.broadcasted_iota(jnp.int32, (8, LB), 0)
    for o in range(nx):
        hit = (sub8 + 8 * o) == target
        tile = jnp.zeros((8, LB), jnp.float32)
        for f, field in enumerate((row, col, one, lane1.astype(jnp.float32))):
            value = jnp.sum(jnp.where(hit, field, 0.0), axis=1, keepdims=True)
            tile = jnp.where(lane8 == f, value, tile)
        plan[o] = tile.astype(jnp.int32)


def plan_of(owners, offsets):
    vm = pl.BlockSpec(memory_space=pltpu.VMEM)
    meta = jnp.pad(jnp.concatenate([owners, offsets], 1).T, ((0, 5), (0, LB - PATS)))
    return pl.pallas_call(
        plan_kernel,
        out_shape=jax.ShapeDtypeStruct((lax.axis_size("tx"), 8, LB), jnp.int32),
        in_specs=[vm],
        out_specs=vm,
        name="plan",
    )(meta)


def mesh_copy(src, dst, s, q, device):
    return pltpu.make_async_remote_copy(
        src_ref=src, dst_ref=dst, send_sem=s, recv_sem=q, device_id=device, device_id_type=pl.DeviceIdType.MESH
    )


def dot(a, b):
    return jnp.dot(a, b, preferred_element_type=jnp.float32)


def update_kernel(
    plan, amp, obj, probe, ta, tb, out, step,
    ext, sbuf, rbuf, ginfo, planm, infom, tpad, den, acc, ps, inv, win, xs, ys,
    d_right, d_below, d_corner, s_right, s_below, s_corner, g_right, g_below, g_corner, ra, sb, rb, gc, gd,
    si, qi, sp, qp, sh, qh, sc, qc, sd, qd, sa, qa, sbs, qb, scs, qcs, sds, qds, ses, qes, sl,
):
    ny, nx = lax.axis_size("ty"), lax.axis_size("tx")
    ty, tx = lax.axis_index("ty"), lax.axis_index("tx")
    down, up = lax.rem(ty + 1, ny), lax.rem(ty + ny - 1, ny)
    east, west = lax.rem(tx + 1, nx), lax.rem(tx + nx - 1, nx)
    barrier = pltpu.get_barrier_semaphore()
    greet = [(ty, lax.rem(tx + d, nx)) for d in range(1, nx)] + [(lax.rem(ty + d, ny), tx) for d in range(1, ny)]
    greet += [(up, west), (down, east)]
    for other in greet:
        pl.semaphore_signal(barrier, inc=1, device_id=other, device_id_type=pl.DeviceIdType.MESH)

    own = []
    for p in range(2):
        for b in range(4):
            own.append(pltpu.make_async_copy(obj.at[p, :, pl.ds(b * LB, LB)], ext.at[p, b, pl.ds(0, T), :], sl.at[len(own)]))
    for copy in own:
        copy.start()
    to_smem = pltpu.make_async_copy(plan, planm, sl.at[8])
    to_smem.start()

    def partner(i, sign):
        d = lax.rem(7 * i, nx)
        y, z = tx // 4, lax.rem(tx, 4)
        dy, dz = d // 4, lax.rem(d, 4)
        return lax.rem(y + nx + sign * dy, nx // 4) * 4 + lax.rem(z + 4 + sign * dz, 4)

    def info_copy(i):
        peer = partner(i, 1)
        return mesh_copy(plan.at[peer], ginfo.at[i], si.at[i - 1], qi.at[i - 1], (ty, peer))

    def amp_copy(m):
        return mesh_copy(sbuf.at[m], rbuf.at[m], sp.at[m], qp.at[m], (ty, partner(lax.rem(m, nx), 1)))

    below = []
    for p in range(2):
        for b in range(4):
            k, lanes = len(below), pl.ds(b * LB, LB)
            below.append(mesh_copy(obj.at[p, pl.ds(0, W), lanes], ext.at[p, b, pl.ds(T, W), :], sh.at[k], qh.at[k], (up, tx)))

    halo = []
    for r in range(2):
        for p in range(2):
            for b in range(2):
                k, at = len(halo), pl.ds(r * W, W)
                part = obj.at[p, at, pl.ds(b * LB, LB)]
                halo.append(mesh_copy(part, ext.at[p, 4 + b, at, :], sc.at[k], qc.at[k], (ty, west)))
    corner = []
    for p in range(2):
        for b in range(2):
            k, part = 8 + len(corner), ext.at[p, 4 + b, pl.ds(0, W), :]
            corner.append(mesh_copy(part, ext.at[p, 4 + b, pl.ds(T, W), :], sc.at[k], qc.at[k], (up, tx)))

    pl.semaphore_wait(barrier, len(greet))
    lax.fori_loop(1, nx, lambda i, c: (info_copy(i).start(), c)[1], 0)
    for pair in zip(halo, below):
        for copy in pair:
            copy.start()
    ginfo[0] = plan[tx]
    to_smem.wait()

    def pack(m, carry):
        i, k = lax.rem(m, nx), m // nx

        @pl.when(i > 0)
        def _():
            sbuf[m] = amp[planm[partner(i, 1), k, 3]]
            amp_copy(m).start()

        @pl.when(i == 0)
        def _():
            rbuf[m] = amp[planm[tx, k, 3]]

        return carry

    lax.fori_loop(0, FIRST, pack, 0)

    for q in range(GROUP):
        for p in range(2):
            for b in range(5):
                tpad[q, p, b] = jnp.zeros((FRAME, LB), jnp.float32)

    def clear(i, carry):
        at = pl.ds(pl.multiple_of(i * CH, CH), CH)
        zero = jnp.zeros((CH, LB), jnp.float32)
        for b in range(SIDE // LB):
            den[b, at, :] = zero
            for p in range(2):
                acc[p, b, at, :] = zero
        return carry

    lax.fori_loop(0, SIDE // CH, clear, 0)
    ps[...] = jnp.zeros(ps.shape, jnp.float32)
    lax.fori_loop(1, nx, lambda i, c: (info_copy(i).wait_recv(), c)[1], 0)
    to_smem = pltpu.make_async_copy(ginfo, infom, sl.at[8])
    to_smem.start()
    to_smem.wait()
    lane = lax.broadcasted_iota(jnp.int32, (RB, LB), 1)

    def windows(g):
        found = []
        for q in range(GROUP):
            m = g * GROUP + q
            i, k = lax.rem(m, nx), m // nx
            found.append((infom[i, k, 0], infom[i, k, 1], infom[i, k, 2].astype(jnp.float32)))
        return found

    def place(q, p, k, halves, cs):
        high = lane >= cs
        a = [pltpu.roll(half, cs, 1) for half in halves]
        at = slice(CH + k, CH + k + RB)
        tpad[q, p, 1, at, :] = jnp.where(high, a[0], 0.0)
        tpad[q, p, 2, at, :] = jnp.where(high, a[1], a[0])
        tpad[q, p, 3, at, :] = jnp.where(high, 0.0, a[1])

    def pull(found, planes):
        cols = [[jnp.clip(b - c // LB, -1, 3) + 1 for b in range(SIDE // LB)] for _, c, _ in found]

        def rows(j, carry):
            y0 = pl.multiple_of(j * CH, CH)
            starts = [jnp.clip(y0 - r, -CH, W) + CH for r, _, _ in found]
            for b in range(SIDE // LB):
                for p, ref in enumerate(planes):
                    v = ref[b, pl.ds(y0, CH), :]
                    for q in range(GROUP):
                        v = v + tpad[q, p, cols[q][b], pl.ds(starts[q], CH), :]
                    ref[b, pl.ds(y0, CH), :] = v
            return carry

        lax.fori_loop(0, SIDE // CH, rows, 0)

    def spread(g, carry):
        found = windows(g)
        for k in range(0, W, RB):
            power = []
            for h in range(2):
                at = slice(h * LB, h * LB + LB)
                pr, pi = probe[0, k:k + RB, at], probe[1, k:k + RB, at]
                power.append(pr * pr + pi * pi)
            for q in range(GROUP):
                place(q, 0, k, [x * found[q][2] for x in power], lax.rem(found[q][1], LB))
        pull(found, [den])
        return carry

    groups = CAP * nx // GROUP
    lax.fori_loop(0, groups, spread, 0)
    d_strips = [
        mesh_copy(den.at[pl.ds(4, 2), pl.ds(0, T), :], d_right, sd.at[0], qd.at[0], (ty, east)),
        mesh_copy(den.at[pl.ds(4, 2), pl.ds(T, W), :], d_corner, sd.at[1], qd.at[1], (down, east)),
        mesh_copy(den.at[pl.ds(0, 4), pl.ds(T, W), :], d_below, sd.at[2], qd.at[2], (down, tx)),
    ]
    for copy in d_strips:
        copy.start()

    for arrived, onward in zip(halo[:4], corner):
        arrived.wait_recv()
        onward.start()
    for copy in own:
        copy.wait()
    for copy in halo[4:] + below + corner:
        copy.wait_recv()

    def half(t, q):
        y = dot(t[...], xs[q]).astype(jnp.bfloat16)
        ys[q, :, :W] = y[:W]
        ys[q, :, W:] = y[W:]

    def group(g, carry):
        found = windows(g)
        for q in range(AHEAD):
            later = FIRST + g * AHEAD + q

            @pl.when(later < CAP * nx)
            def _():
                pack(later, 0)

        for q in range(GROUP):
            m = g * GROUP + q

            @pl.when(lax.rem(m, nx) > 0)
            def _():
                amp_copy(m).wait_recv()

        for q in range(GROUP):
            r, c, _ = found[q]
            cb, cs = c // LB, lax.rem(c, LB)
            back = lax.rem(LB - cs, LB)
            low = lane < LB - cs
            for k in range(0, W, RB):
                o = []
                for p in range(2):
                    b = [pltpu.roll(ext[p, cb + j, pl.ds(r + k, RB), :], back, 1) for j in range(3)]
                    o.append([jnp.where(low, b[0], b[1]), jnp.where(low, b[1], b[2])])
                for h in range(2):
                    at = slice(h * LB, h * LB + LB)
                    ore, oim = o[0][h], o[1][h]
                    win[q, 0, k:k + RB, at] = ore
                    win[q, 1, k:k + RB, at] = oim
                    pr, pi = probe[0, k:k + RB, at], probe[1, k:k + RB, at]
                    xs[q, k:k + RB, at] = (pr * ore - pi * oim).astype(jnp.bfloat16)
                    xs[q, W + k:W + k + RB, at] = (pr * oim + pi * ore).astype(jnp.bfloat16)
        for q in range(GROUP):
            half(ta, q)
        for q in range(GROUP):
            z = dot(ys[q], tb[...])
            zr, zi = z[:, :W], z[:, W:]
            f = rbuf[g * GROUP + q].astype(jnp.float32) * lax.rsqrt(zr * zr + zi * zi + 0.01)
            xs[q, :W] = (zr * f).astype(jnp.bfloat16)
            xs[q, W:] = (zi * f).astype(jnp.bfloat16)
        for q in range(GROUP):
            half(tb, q)
        zs = [dot(ys[q], ta[...]) for q in range(GROUP)]
        for k in range(0, W, RB):
            terms = [[[], []] for q in range(GROUP)]
            for h in range(2):
                at = slice(h * LB, h * LB + LB)
                pr, pi = probe[0, k:k + RB, at], probe[1, k:k + RB, at]
                sums = None
                for q in range(GROUP):
                    live = found[q][2]
                    ore, oim = win[q, 0, k:k + RB, at], win[q, 1, k:k + RB, at]
                    dr = (zs[q][k:k + RB, at] - (pr * ore - pi * oim)) * live
                    di = (zs[q][k:k + RB, W + h * LB:W + h * LB + LB] - (pr * oim + pi * ore)) * live
                    terms[q][0].append(pr * dr + pi * di)
                    terms[q][1].append(pr * di - pi * dr)
                    mine = (ore * dr + oim * di, ore * di - oim * dr, (ore * ore + oim * oim) * live)
                    sums = mine if sums is None else tuple(x + y for x, y in zip(sums, mine))
                for j in range(3):
                    ps[j, k:k + RB, at] += sums[j]
            for q in range(GROUP):
                for p in range(2):
                    place(q, p, k, terms[q][p], lax.rem(found[q][1], LB))
        pull(found, [acc.at[0], acc.at[1]])
        return carry

    lax.fori_loop(0, groups, group, 0)

    def send(*args):
        copy = mesh_copy(*args)
        copy.start()
        return copy

    rows = W // ny
    stage_a = []
    for d in range(1, ny):
        peer = lax.rem(ty + d, ny)
        piece = ps.at[:, pl.ds(pl.multiple_of(peer * rows, rows), rows), :]
        stage_a.append(send(piece, ra.at[ty], sa.at[d - 1], qa.at[d - 1], (peer, tx)))
    strips = []

    def strip(kind, p, b):
        k = len(strips)
        if kind == 0:
            s_right[p, b] = acc[p, 4 + b, :T, :].astype(jnp.bfloat16)
            strips.append(send(s_right.at[p, b], g_right.at[p, b], ses.at[k], qes.at[k], (ty, east)))
        elif kind == 1:
            s_corner[p, b] = acc[p, 4 + b, T:, :].astype(jnp.bfloat16)
            strips.append(send(s_corner.at[p, b], g_corner.at[p, b], ses.at[k], qes.at[k], (down, east)))
        else:
            s_below[p, b] = acc[p, b, T:, :].astype(jnp.bfloat16)
            strips.append(send(s_below.at[p, b], g_below.at[p, b], ses.at[k], qes.at[k], (down, tx)))

    for what in ((0, 0, 0), (2, 0, 0), (0, 0, 1), (2, 0, 1), (0, 1, 0), (2, 0, 2)):
        strip(*what)
    ra[ty] = ps[:, pl.ds(pl.multiple_of(ty * rows, rows), rows), :]

    for copy in d_strips:
        copy.wait_recv()
    has_west = jnp.where(tx > 0, 1.0, 0.0)
    has_north = jnp.where(ty > 0, 1.0, 0.0)
    has_both = has_west * has_north
    for b in range(4):
        top, rest = den[b, :W, :] + has_north * d_below[b], den[b, W:T, :]
        if b < 2:
            top = top + (has_west * d_right[b, :W, :] + has_both * d_corner[b])
            rest = rest + has_west * d_right[b, W:, :]
        inv[b, :W, :] = 1.0 / (top + 1.0)
        inv[b, W:, :] = 1.0 / (rest + 1.0)

    for copy in stage_a:
        copy.wait_recv()
    total = ra[0]
    for j in range(1, ny):
        total = total + ra[j]
    for j in range(nx):
        p, g, h = j // (nx // 2), j // 2 % (rows // 8), j % 2
        lanes = slice(h * LB, h * LB + LB)
        sb[j, 0] = total[p, g * 8:g * 8 + 8, lanes]
        sb[j, 1] = total[2, g * 8:g * 8 + 8, lanes]
    stage_b = []
    for d in range(1, nx):
        peer = lax.rem(tx + d, nx)
        stage_b.append(send(sb.at[peer], rb.at[tx], sbs.at[d - 1], qb.at[d - 1], (ty, peer)))
    rb[tx] = sb[tx]
    for what in ((0, 1, 1), (2, 0, 3), (1, 0, 0)):
        strip(*what)
    for copy in stage_b:
        copy.wait_recv()
    total = rb[0]
    for j in range(1, nx):
        total = total + rb[j]
    gc[tx] = total[0] / jnp.sqrt(total[1] + 1.0)
    stage_c = []
    for d in range(1, nx):
        peer = lax.rem(tx + d, nx)
        stage_c.append(send(gc.at[tx], gc.at[tx], scs.at[d - 1], qcs.at[d - 1], (ty, peer)))
    for what in ((1, 0, 1), (2, 1, 0), (1, 1, 0), (2, 1, 1), (1, 1, 1)):
        strip(*what)
    for copy in stage_c:
        copy.wait_recv()
    gd[ty] = gc[...]
    stage_d = []
    for d in range(1, ny):
        peer = lax.rem(ty + d, ny)
        stage_d.append(send(gc, gd.at[ty], sds.at[d - 1], qds.at[d - 1], (peer, tx)))

    for what in ((2, 1, 2), (2, 1, 3)):
        strip(*what)
    for copy in strips:
        copy.wait_recv()

    def upper(i, carry):
        at = pl.ds(pl.multiple_of(i * RB, RB), RB)
        for b in range(4):
            lanes = slice(b * LB, b * LB + LB)
            for p in range(2):
                num = acc[p, b, at, :] + has_north * g_below[p, b, at, :].astype(jnp.float32)
                if b < 2:
                    num = num + has_west * g_right[p, b, at, :].astype(jnp.float32)
                    num = num + has_both * g_corner[p, b, at, :].astype(jnp.float32)
                out[p, at, lanes] = ext[p, b, at, :] + num * inv[b, at, :]
        return carry

    def lower(i, carry):
        at = pl.ds(pl.multiple_of(i * RB, RB), RB)
        for b in range(4):
            lanes = slice(b * LB, b * LB + LB)
            for p in range(2):
                num = acc[p, b, at, :]
                if b < 2:
                    num = num + has_west * g_right[p, b, at, :].astype(jnp.float32)
                out[p, at, lanes] = ext[p, b, at, :] + num * inv[b, at, :]
        return carry

    lax.fori_loop(0, W // RB, upper, 0)
    lax.fori_loop(W // RB, T // RB, lower, 0)

    for copy in stage_d:
        copy.wait_recv()
    for t in range(ny):
        for j in range(nx):
            p, g, h = j // (nx // 2), j // 2 % (rows // 8), j % 2
            step[p, t * rows + g * 8:t * rows + g * 8 + 8, h * LB:h * LB + LB] = gd[t, j]
    for copy in halo + below + corner + d_strips + stage_a + strips + stage_b + stage_c + stage_d:
        copy.wait_send()
    lax.fori_loop(1, nx, lambda i, c: (info_copy(i).wait_send(), c)[1], 0)

    def sent(m, carry):
        @pl.when(lax.rem(m, nx) > 0)
        def _():
            amp_copy(m).wait_send()

        return carry

    lax.fori_loop(0, CAP * nx, sent, 0)


def update(plan, amp, obj, probe, ta, tb):
    ny, nx = lax.axis_size("ty"), lax.axis_size("tx")
    vm = pl.BlockSpec(memory_space=pltpu.VMEM)
    bf, f32, i32 = jnp.bfloat16, jnp.float32, jnp.int32
    dma = pltpu.SemaphoreType.DMA
    blocks = SIDE // LB
    strips = [(2, 2, T, LB), (2, 4, W, LB), (2, 2, W, LB)]
    sems = [nx - 1, nx - 1, CAP * nx, CAP * nx, 8, 8, 12, 12, 3, 3]
    sems += [ny - 1, ny - 1, nx - 1, nx - 1, nx - 1, nx - 1, ny - 1, ny - 1, 16, 16, 9]
    return pl.pallas_call(
        update_kernel,
        out_shape=(jax.ShapeDtypeStruct(obj.shape, f32), jax.ShapeDtypeStruct((2, W, W), f32)),
        in_specs=[vm, vm, pl.BlockSpec(memory_space=pl.ANY), vm, vm, vm],
        out_specs=(vm, vm),
        scratch_shapes=[
            pltpu.VMEM((2, blocks, SIDE, LB), f32),
            pltpu.VMEM((CAP * nx, W, W), bf),
            pltpu.VMEM((CAP * nx, W, W), bf),
            pltpu.VMEM((nx, 8, LB), i32),
            pltpu.SMEM((nx, 8, LB), i32),
            pltpu.SMEM((nx, 8, LB), i32),
            pltpu.VMEM((GROUP, 2, 5, FRAME, LB), f32),
            pltpu.VMEM((blocks, SIDE, LB), f32),
            pltpu.VMEM((2, blocks, SIDE, LB), f32),
            pltpu.VMEM((3, W, W), f32),
            pltpu.VMEM((4, T, LB), f32),
            pltpu.VMEM((GROUP, 2, W, W), f32),
            pltpu.VMEM((GROUP, 2 * W, W), bf),
            pltpu.VMEM((GROUP, W, 2 * W), bf),
        ]
        + [pltpu.VMEM(x[1:], f32) for x in strips]
        + [pltpu.VMEM(x, bf) for x in strips + strips]
        + [
            pltpu.VMEM((ny, 3, W // ny, W), f32),
            pltpu.VMEM((nx, 2, 8, LB), f32),
            pltpu.VMEM((nx, 2, 8, LB), f32),
            pltpu.VMEM((nx, 8, LB), f32),
            pltpu.VMEM((ny, nx, 8, LB), f32),
        ]
        + [dma((k,)) for k in sems],
        compiler_params=pltpu.CompilerParams(vmem_limit_bytes=60 * MIB, collective_id=0, has_side_effects=True),
        name="update",
    )(plan, amp, obj, probe, ta, tb)


def local(amplitudes, owners, offsets, object_field, probe):
    plan = plan_of(owners, offsets)
    ta, tb = tables()
    return update(plan, amplitudes, object_field, probe, ta, tb)


def solution(mesh):
    return jax.shard_map(
        local,
        mesh=mesh,
        in_specs=(
            P(("ty", "tx"), None, None),
            P(("ty", "tx"), None),
            P(("ty", "tx"), None),
            P(None, "ty", "tx"),
            P(),
        ),
        out_specs=(P(None, "ty", "tx"), P()),
        check_vma=False,
    )
```

```python
import functools
import math

import jax
import jax.numpy as jnp
import ml_dtypes
import numpy as np
from jax import lax
from jax.experimental import pallas as pl
from jax.experimental.pallas import tpu as pltpu
from jax.sharding import PartitionSpec as P

W = 256
T = 512
SIDE = T + W
CAP = 3
PATS = 32
GROUP = 3
FIRST = 12
AHEAD = 3
CH = 64
FRAME = W + 2 * CH
RB = 32
LB = 128
MIB = 2**20


def tables():
    steps = np.arange(W)
    phase = (steps[:, None] * steps[None, :] % W).astype(np.float32)
    angles = phase * np.float32(2.0 * math.pi / W)
    c, s = np.cos(angles) / np.float32(math.sqrt(W)), np.sin(angles) / np.float32(math.sqrt(W))
    ta, tb = np.block([[c, s], [-s, c]]), np.block([[c, -s], [s, c]])
    return jnp.asarray(ta.astype(ml_dtypes.bfloat16)), jnp.asarray(tb.astype(ml_dtypes.bfloat16))


def plan_kernel(meta, plan):
    ny, nx = lax.axis_size("ty"), lax.axis_size("tx")
    ty = lax.axis_index("ty")
    owner, row, col = meta[0:1, :], meta[1:2, :], meta[2:3, :]
    lane1 = lax.broadcasted_iota(jnp.int32, (1, LB), 1)
    rank = jnp.zeros((1, LB), jnp.int32)
    for d in range(1, PATS):
        rank = rank + jnp.where((pltpu.roll(owner, d, 1) == owner) & (lane1 >= d), 1, 0)
    target = jnp.where(lane1 < PATS, owner * 8 + rank, -1)
    row = jnp.minimum(row, ny * T - W - ty * T).astype(jnp.float32)
    col = jnp.minimum(col, nx * T - W - owner * T).astype(jnp.float32)
    one = jnp.ones((1, LB), jnp.float32)
    lane8 = lax.broadcasted_iota(jnp.int32, (8, LB), 1)
    sub8 = lax.broadcasted_iota(jnp.int32, (8, LB), 0)
    for o in range(nx):
        hit = (sub8 + 8 * o) == target
        tile = jnp.zeros((8, LB), jnp.float32)
        for f, field in enumerate((row, col, one, lane1.astype(jnp.float32))):
            value = jnp.sum(jnp.where(hit, field, 0.0), axis=1, keepdims=True)
            tile = jnp.where(lane8 == f, value, tile)
        plan[o] = tile.astype(jnp.int32)


def plan_of(owners, offsets):
    vm = pl.BlockSpec(memory_space=pltpu.VMEM)
    meta = jnp.pad(jnp.concatenate([owners, offsets], 1).T, ((0, 5), (0, LB - PATS)))
    return pl.pallas_call(
        plan_kernel,
        out_shape=jax.ShapeDtypeStruct((lax.axis_size("tx"), 8, LB), jnp.int32),
        in_specs=[vm],
        out_specs=vm,
        name="plan",
    )(meta)


def mesh_copy(src, dst, s, q, device):
    return pltpu.make_async_remote_copy(
        src_ref=src, dst_ref=dst, send_sem=s, recv_sem=q, device_id=device, device_id_type=pl.DeviceIdType.MESH
    )


def dot(a, b):
    return jnp.dot(a, b, preferred_element_type=jnp.float32)


def update_kernel(
    plan, amp, obj, probe, ta, tb, out, step,
    ext, sbuf, rbuf, ginfo, planm, infom, tpad, den, acc, ps, inv, win, xs, ys,
    d_right, d_below, d_corner, s_right, s_below, s_corner, g_right, g_below, g_corner, ra, sb, rb, gc, gd,
    si, qi, sp, qp, sh, qh, sc, qc, sd, qd, sa, qa, sbs, qb, scs, qcs, sds, qds, ses, qes, sl,
):
    ny, nx = lax.axis_size("ty"), lax.axis_size("tx")
    ty, tx = lax.axis_index("ty"), lax.axis_index("tx")
    down, up = lax.rem(ty + 1, ny), lax.rem(ty + ny - 1, ny)
    east, west = lax.rem(tx + 1, nx), lax.rem(tx + nx - 1, nx)
    barrier = pltpu.get_barrier_semaphore()
    greet = [(ty, lax.rem(tx + d, nx)) for d in range(1, nx)] + [(lax.rem(ty + d, ny), tx) for d in range(1, ny)]
    greet += [(up, west), (down, east)]
    for other in greet:
        pl.semaphore_signal(barrier, inc=1, device_id=other, device_id_type=pl.DeviceIdType.MESH)

    own = []
    for p in range(2):
        for b in range(4):
            own.append(pltpu.make_async_copy(obj.at[p, :, pl.ds(b * LB, LB)], ext.at[p, b, pl.ds(0, T), :], sl.at[len(own)]))
    for copy in own:
        copy.start()
    to_smem = pltpu.make_async_copy(plan, planm, sl.at[8])
    to_smem.start()

    def partner(i, sign):
        d = lax.rem(9 * i, nx)
        y, z = tx // 4, lax.rem(tx, 4)
        dy, dz = d // 4, lax.rem(d, 4)
        return lax.rem(y + nx + sign * dy, nx // 4) * 4 + lax.rem(z + 4 + sign * dz, 4)

    def info_copy(i):
        peer = partner(i, 1)
        return mesh_copy(plan.at[peer], ginfo.at[i], si.at[i - 1], qi.at[i - 1], (ty, peer))

    def amp_copy(m):
        return mesh_copy(sbuf.at[m], rbuf.at[m], sp.at[m], qp.at[m], (ty, partner(lax.rem(m, nx), 1)))

    below = []
    for p in range(2):
        for b in range(4):
            k, lanes = len(below), pl.ds(b * LB, LB)
            below.append(mesh_copy(obj.at[p, pl.ds(0, W), lanes], ext.at[p, b, pl.ds(T, W), :], sh.at[k], qh.at[k], (up, tx)))

    halo = []
    for r in range(2):
        for p in range(2):
            for b in range(2):
                k, at = len(halo), pl.ds(r * W, W)
                part = obj.at[p, at, pl.ds(b * LB, LB)]
                halo.append(mesh_copy(part, ext.at[p, 4 + b, at, :], sc.at[k], qc.at[k], (ty, west)))
    corner = []
    for p in range(2):
        for b in range(2):
            k, part = 8 + len(corner), ext.at[p, 4 + b, pl.ds(0, W), :]
            corner.append(mesh_copy(part, ext.at[p, 4 + b, pl.ds(T, W), :], sc.at[k], qc.at[k], (up, tx)))

    pl.semaphore_wait(barrier, len(greet))
    lax.fori_loop(1, nx, lambda i, c: (info_copy(i).start(), c)[1], 0)
    for pair in zip(halo, below):
        for copy in pair:
            copy.start()
    ginfo[0] = plan[tx]
    to_smem.wait()

    def pack(m, carry):
        i, k = lax.rem(m, nx), m // nx

        @pl.when(i > 0)
        def _():
            sbuf[m] = amp[planm[partner(i, 1), k, 3]]
            amp_copy(m).start()

        @pl.when(i == 0)
        def _():
            rbuf[m] = amp[planm[tx, k, 3]]

        return carry

    lax.fori_loop(0, FIRST, pack, 0)

    for q in range(GROUP):
        for p in range(2):
            for b in range(5):
                tpad[q, p, b] = jnp.zeros((FRAME, LB), jnp.float32)

    def clear(i, carry):
        at = pl.ds(pl.multiple_of(i * CH, CH), CH)
        zero = jnp.zeros((CH, LB), jnp.float32)
        for b in range(SIDE // LB):
            den[b, at, :] = zero
            for p in range(2):
                acc[p, b, at, :] = zero
        return carry

    lax.fori_loop(0, SIDE // CH, clear, 0)
    ps[...] = jnp.zeros(ps.shape, jnp.float32)
    lax.fori_loop(1, nx, lambda i, c: (info_copy(i).wait_recv(), c)[1], 0)
    to_smem = pltpu.make_async_copy(ginfo, infom, sl.at[8])
    to_smem.start()
    to_smem.wait()
    lane = lax.broadcasted_iota(jnp.int32, (RB, LB), 1)

    def windows(g):
        found = []
        for q in range(GROUP):
            m = g * GROUP + q
            i, k = lax.rem(m, nx), m // nx
            found.append((infom[i, k, 0], infom[i, k, 1], infom[i, k, 2].astype(jnp.float32)))
        return found

    def place(q, p, k, halves, cs):
        high = lane >= cs
        a = [pltpu.roll(half, cs, 1) for half in halves]
        at = slice(CH + k, CH + k + RB)
        tpad[q, p, 1, at, :] = jnp.where(high, a[0], 0.0)
        tpad[q, p, 2, at, :] = jnp.where(high, a[1], a[0])
        tpad[q, p, 3, at, :] = jnp.where(high, 0.0, a[1])

    def pull(found, planes):
        cols = [[jnp.clip(b - c // LB, -1, 3) + 1 for b in range(SIDE // LB)] for _, c, _ in found]

        def rows(j, carry):
            y0 = pl.multiple_of(j * CH, CH)
            starts = [jnp.clip(y0 - r, -CH, W) + CH for r, _, _ in found]
            for b in range(SIDE // LB):
                for p, ref in enumerate(planes):
                    v = ref[b, pl.ds(y0, CH), :]
                    for q in range(GROUP):
                        v = v + tpad[q, p, cols[q][b], pl.ds(starts[q], CH), :]
                    ref[b, pl.ds(y0, CH), :] = v
            return carry

        lax.fori_loop(0, SIDE // CH, rows, 0)

    def spread(g, carry):
        found = windows(g)
        for k in range(0, W, RB):
            power = []
            for h in range(2):
                at = slice(h * LB, h * LB + LB)
                pr, pi = probe[0, k:k + RB, at], probe[1, k:k + RB, at]
                power.append(pr * pr + pi * pi)
            for q in range(GROUP):
                place(q, 0, k, [x * found[q][2] for x in power], lax.rem(found[q][1], LB))
        pull(found, [den])
        return carry

    groups = CAP * nx // GROUP
    lax.fori_loop(0, groups, spread, 0)
    d_strips = [
        mesh_copy(den.at[pl.ds(4, 2), pl.ds(0, T), :], d_right, sd.at[0], qd.at[0], (ty, east)),
        mesh_copy(den.at[pl.ds(4, 2), pl.ds(T, W), :], d_corner, sd.at[1], qd.at[1], (down, east)),
        mesh_copy(den.at[pl.ds(0, 4), pl.ds(T, W), :], d_below, sd.at[2], qd.at[2], (down, tx)),
    ]
    for copy in d_strips:
        copy.start()

    for arrived, onward in zip(halo[:4], corner):
        arrived.wait_recv()
        onward.start()
    for copy in own:
        copy.wait()
    for copy in halo[4:] + below + corner:
        copy.wait_recv()

    def half(t, q):
        y = dot(t[...], xs[q]).astype(jnp.bfloat16)
        ys[q, :, :W] = y[:W]
        ys[q, :, W:] = y[W:]

    def group(g, carry):
        found = windows(g)
        for q in range(AHEAD):
            later = FIRST + g * AHEAD + q

            @pl.when(later < CAP * nx)
            def _():
                pack(later, 0)

        for q in range(GROUP):
            m = g * GROUP + q

            @pl.when(lax.rem(m, nx) > 0)
            def _():
                amp_copy(m).wait_recv()

        for q in range(GROUP):
            r, c, _ = found[q]
            cb, cs = c // LB, lax.rem(c, LB)
            back = lax.rem(LB - cs, LB)
            low = lane < LB - cs
            for k in range(0, W, RB):
                o = []
                for p in range(2):
                    b = [pltpu.roll(ext[p, cb + j, pl.ds(r + k, RB), :], back, 1) for j in range(3)]
                    o.append([jnp.where(low, b[0], b[1]), jnp.where(low, b[1], b[2])])
                for h in range(2):
                    at = slice(h * LB, h * LB + LB)
                    ore, oim = o[0][h], o[1][h]
                    win[q, 0, k:k + RB, at] = ore
                    win[q, 1, k:k + RB, at] = oim
                    pr, pi = probe[0, k:k + RB, at], probe[1, k:k + RB, at]
                    xs[q, k:k + RB, at] = (pr * ore - pi * oim).astype(jnp.bfloat16)
                    xs[q, W + k:W + k + RB, at] = (pr * oim + pi * ore).astype(jnp.bfloat16)
        for q in range(GROUP):
            half(ta, q)
        for q in range(GROUP):
            z = dot(ys[q], tb[...])
            zr, zi = z[:, :W], z[:, W:]
            f = rbuf[g * GROUP + q].astype(jnp.float32) * lax.rsqrt(zr * zr + zi * zi + 0.01)
            xs[q, :W] = (zr * f).astype(jnp.bfloat16)
            xs[q, W:] = (zi * f).astype(jnp.bfloat16)
        for q in range(GROUP):
            half(tb, q)
        zs = [dot(ys[q], ta[...]) for q in range(GROUP)]
        for k in range(0, W, RB):
            terms = [[[], []] for q in range(GROUP)]
            for h in range(2):
                at = slice(h * LB, h * LB + LB)
                pr, pi = probe[0, k:k + RB, at], probe[1, k:k + RB, at]
                sums = None
                for q in range(GROUP):
                    live = found[q][2]
                    ore, oim = win[q, 0, k:k + RB, at], win[q, 1, k:k + RB, at]
                    dr = (zs[q][k:k + RB, at] - (pr * ore - pi * oim)) * live
                    di = (zs[q][k:k + RB, W + h * LB:W + h * LB + LB] - (pr * oim + pi * ore)) * live
                    terms[q][0].append(pr * dr + pi * di)
                    terms[q][1].append(pr * di - pi * dr)
                    mine = (ore * dr + oim * di, ore * di - oim * dr, (ore * ore + oim * oim) * live)
                    sums = mine if sums is None else tuple(x + y for x, y in zip(sums, mine))
                for j in range(3):
                    ps[j, k:k + RB, at] += sums[j]
            for q in range(GROUP):
                for p in range(2):
                    place(q, p, k, terms[q][p], lax.rem(found[q][1], LB))
        pull(found, [acc.at[0], acc.at[1]])
        return carry

    lax.fori_loop(0, groups, group, 0)

    def send(*args):
        copy = mesh_copy(*args)
        copy.start()
        return copy

    rows = W // ny
    stage_a = []
    for d in range(1, ny):
        peer = lax.rem(ty + d, ny)
        piece = ps.at[:, pl.ds(pl.multiple_of(peer * rows, rows), rows), :]
        stage_a.append(send(piece, ra.at[ty], sa.at[d - 1], qa.at[d - 1], (peer, tx)))
    strips = []

    def strip(kind, p, b):
        k = len(strips)
        if kind == 0:
            s_right[p, b] = acc[p, 4 + b, :T, :].astype(jnp.bfloat16)
            strips.append(send(s_right.at[p, b], g_right.at[p, b], ses.at[k], qes.at[k], (ty, east)))
        elif kind == 1:
            s_corner[p, b] = acc[p, 4 + b, T:, :].astype(jnp.bfloat16)
            strips.append(send(s_corner.at[p, b], g_corner.at[p, b], ses.at[k], qes.at[k], (down, east)))
        else:
            s_below[p, b] = acc[p, b, T:, :].astype(jnp.bfloat16)
            strips.append(send(s_below.at[p, b], g_below.at[p, b], ses.at[k], qes.at[k], (down, tx)))

    for what in ((0, 0, 0), (2, 0, 0), (0, 0, 1), (2, 0, 1), (0, 1, 0), (2, 0, 2)):
        strip(*what)
    ra[ty] = ps[:, pl.ds(pl.multiple_of(ty * rows, rows), rows), :]

    for copy in d_strips:
        copy.wait_recv()
    has_west = jnp.where(tx > 0, 1.0, 0.0)
    has_north = jnp.where(ty > 0, 1.0, 0.0)
    has_both = has_west * has_north
    for b in range(4):
        top, rest = den[b, :W, :] + has_north * d_below[b], den[b, W:T, :]
        if b < 2:
            top = top + (has_west * d_right[b, :W, :] + has_both * d_corner[b])
            rest = rest + has_west * d_right[b, W:, :]
        inv[b, :W, :] = 1.0 / (top + 1.0)
        inv[b, W:, :] = 1.0 / (rest + 1.0)

    for copy in stage_a:
        copy.wait_recv()
    total = ra[0]
    for j in range(1, ny):
        total = total + ra[j]
    for j in range(nx):
        p, g, h = j // (nx // 2), j // 2 % (rows // 8), j % 2
        lanes = slice(h * LB, h * LB + LB)
        sb[j, 0] = total[p, g * 8:g * 8 + 8, lanes]
        sb[j, 1] = total[2, g * 8:g * 8 + 8, lanes]
    stage_b = []
    for d in range(1, nx):
        peer = lax.rem(tx + d, nx)
        stage_b.append(send(sb.at[peer], rb.at[tx], sbs.at[d - 1], qb.at[d - 1], (ty, peer)))
    rb[tx] = sb[tx]
    for what in ((0, 1, 1), (2, 0, 3), (1, 0, 0)):
        strip(*what)
    for copy in stage_b:
        copy.wait_recv()
    total = rb[0]
    for j in range(1, nx):
        total = total + rb[j]
    gc[tx] = total[0] / jnp.sqrt(total[1] + 1.0)
    stage_c = []
    for d in range(1, nx):
        peer = lax.rem(tx + d, nx)
        stage_c.append(send(gc.at[tx], gc.at[tx], scs.at[d - 1], qcs.at[d - 1], (ty, peer)))
    for what in ((1, 0, 1), (2, 1, 0), (1, 1, 0), (2, 1, 1), (1, 1, 1)):
        strip(*what)
    for copy in stage_c:
        copy.wait_recv()
    gd[ty] = gc[...]
    stage_d = []
    for d in range(1, ny):
        peer = lax.rem(ty + d, ny)
        stage_d.append(send(gc, gd.at[ty], sds.at[d - 1], qds.at[d - 1], (peer, tx)))

    for what in ((2, 1, 2), (2, 1, 3)):
        strip(*what)
    for copy in strips:
        copy.wait_recv()

    def upper(i, carry):
        at = pl.ds(pl.multiple_of(i * RB, RB), RB)
        for b in range(4):
            lanes = slice(b * LB, b * LB + LB)
            for p in range(2):
                num = acc[p, b, at, :] + has_north * g_below[p, b, at, :].astype(jnp.float32)
                if b < 2:
                    num = num + has_west * g_right[p, b, at, :].astype(jnp.float32)
                    num = num + has_both * g_corner[p, b, at, :].astype(jnp.float32)
                out[p, at, lanes] = ext[p, b, at, :] + num * inv[b, at, :]
        return carry

    def lower(i, carry):
        at = pl.ds(pl.multiple_of(i * RB, RB), RB)
        for b in range(4):
            lanes = slice(b * LB, b * LB + LB)
            for p in range(2):
                num = acc[p, b, at, :]
                if b < 2:
                    num = num + has_west * g_right[p, b, at, :].astype(jnp.float32)
                out[p, at, lanes] = ext[p, b, at, :] + num * inv[b, at, :]
        return carry

    lax.fori_loop(0, W // RB, upper, 0)
    lax.fori_loop(W // RB, T // RB, lower, 0)

    for copy in stage_d:
        copy.wait_recv()
    for t in range(ny):
        for j in range(nx):
            p, g, h = j // (nx // 2), j // 2 % (rows // 8), j % 2
            step[p, t * rows + g * 8:t * rows + g * 8 + 8, h * LB:h * LB + LB] = gd[t, j]
    for copy in halo + below + corner + d_strips + stage_a + strips + stage_b + stage_c + stage_d:
        copy.wait_send()
    lax.fori_loop(1, nx, lambda i, c: (info_copy(i).wait_send(), c)[1], 0)

    def sent(m, carry):
        @pl.when(lax.rem(m, nx) > 0)
        def _():
            amp_copy(m).wait_send()

        return carry

    lax.fori_loop(0, CAP * nx, sent, 0)


def update(plan, amp, obj, probe, ta, tb):
    ny, nx = lax.axis_size("ty"), lax.axis_size("tx")
    vm = pl.BlockSpec(memory_space=pltpu.VMEM)
    bf, f32, i32 = jnp.bfloat16, jnp.float32, jnp.int32
    dma = pltpu.SemaphoreType.DMA
    blocks = SIDE // LB
    strips = [(2, 2, T, LB), (2, 4, W, LB), (2, 2, W, LB)]
    sems = [nx - 1, nx - 1, CAP * nx, CAP * nx, 8, 8, 12, 12, 3, 3]
    sems += [ny - 1, ny - 1, nx - 1, nx - 1, nx - 1, nx - 1, ny - 1, ny - 1, 16, 16, 9]
    return pl.pallas_call(
        update_kernel,
        out_shape=(jax.ShapeDtypeStruct(obj.shape, f32), jax.ShapeDtypeStruct((2, W, W), f32)),
        in_specs=[vm, vm, pl.BlockSpec(memory_space=pl.ANY), vm, vm, vm],
        out_specs=(vm, vm),
        scratch_shapes=[
            pltpu.VMEM((2, blocks, SIDE, LB), f32),
            pltpu.VMEM((CAP * nx, W, W), bf),
            pltpu.VMEM((CAP * nx, W, W), bf),
            pltpu.VMEM((nx, 8, LB), i32),
            pltpu.SMEM((nx, 8, LB), i32),
            pltpu.SMEM((nx, 8, LB), i32),
            pltpu.VMEM((GROUP, 2, 5, FRAME, LB), f32),
            pltpu.VMEM((blocks, SIDE, LB), f32),
            pltpu.VMEM((2, blocks, SIDE, LB), f32),
            pltpu.VMEM((3, W, W), f32),
            pltpu.VMEM((4, T, LB), f32),
            pltpu.VMEM((GROUP, 2, W, W), f32),
            pltpu.VMEM((GROUP, 2 * W, W), bf),
            pltpu.VMEM((GROUP, W, 2 * W), bf),
        ]
        + [pltpu.VMEM(x[1:], f32) for x in strips]
        + [pltpu.VMEM(x, bf) for x in strips + strips]
        + [
            pltpu.VMEM((ny, 3, W // ny, W), f32),
            pltpu.VMEM((nx, 2, 8, LB), f32),
            pltpu.VMEM((nx, 2, 8, LB), f32),
            pltpu.VMEM((nx, 8, LB), f32),
            pltpu.VMEM((ny, nx, 8, LB), f32),
        ]
        + [dma((k,)) for k in sems],
        compiler_params=pltpu.CompilerParams(vmem_limit_bytes=60 * MIB, collective_id=0, has_side_effects=True),
        name="update",
    )(plan, amp, obj, probe, ta, tb)


def local(amplitudes, owners, offsets, object_field, probe):
    plan = plan_of(owners, offsets)
    ta, tb = tables()
    return update(plan, amplitudes, object_field, probe, ta, tb)


def solution(mesh):
    return jax.shard_map(
        local,
        mesh=mesh,
        in_specs=(
            P(("ty", "tx"), None, None),
            P(("ty", "tx"), None),
            P(("ty", "tx"), None),
            P(None, "ty", "tx"),
            P(),
        ),
        out_specs=(P(None, "ty", "tx"), P()),
        check_vma=False,
    )
```
